32 devices in a mesh: req: 4 (over x, core), tp: 8 (over z, y).
Axes of the slice: x: 2, y: 2, z: 4, core: 2. Of those that a mesh axis runs over, the one named last changes fastest.
Arguments:
- hidden: bfloat16 [4, 320, 5120], P('req'), may hold values from -6 to 6
- norm_gain: float32 [5120], replicated, may hold values from 0.5 to 2
- q_weight: float32 [5120, 1024], P(('req', 'tp')), may hold values from -0.078125 to 0.078125
- k_weight: float32 [5120, 1024], P(('req', 'tp')), may hold values from -0.078125 to 0.078125
- v_weight: float32 [5120, 1024], P(('req', 'tp')), may hold values from -0.078125 to 0.078125
- o_weight: float32 [5120, 1024], P(('req', 'tp')), may hold values from -0.5 to 0.5
- key_cache: bfloat16 [4, 512, 1024], P('req', None, 'tp'), may hold values from -160 to 160
- value_cache: bfloat16 [4, 512, 1024], P('req', None, 'tp'), may hold values from -6 to 6
- text_rows: bfloat16 [4, 256, 5120], P('req', 'tp'), may hold values from -6 to 6
- text_index: int32 [4, 256], P('req'), may hold values from 0 to 511, as said below
- clip_len: int32 [4], P('req'), may hold values from 80 to 320, as said below
- text_len: int32 [4], P('req'), may hold values from 128 to 512, as said below
Outputs:
- output: bfloat16 [4, 320, 5120], P('req', 'tp')
The draws below stay inside these ranges and needn't reach their ends.
Inputs may be any that keep to these rules, and one draw needn't show every extreme that they name: `text_index`: within a clip the entries are distinct text rows; clip 0 always recomputes rows 0 and 511. `clip_len`: some clip has exactly 320 live slots and some clip exactly 80. `text_len`: some clip has all 512 text rows live and some clip exactly 128.
All inputs are finite; a program needn't handle non-finite values.
Results may differ from the reference program's by a relative error of at most 0.012.
The reference program's roundings to bfloat16 on the way count: a program that leaves them out, or rounds other values in their place, can miss the bound.
Values may be sent and summed in bfloat16 or wider, within the bound.
A program may use at most 64 MiB of HBM per device.

```python
import math
import jax
import jax.numpy as jnp
from jax import lax

D = 5120
HD = 128
TEXT = 512
LMAX = 320
RECOMP = 256
HEADS = 8
INNER = 1024
CLIPS = 4


def draw_key_cache(key, part):
    full = jnp.clip(jax.random.normal(key, (CLIPS, TEXT, INNER), jnp.float32), -6.0, 6.0) * 1.5
    return full.astype(jnp.bfloat16)


def draw_text_index(key, part):
    keys = jax.random.split(key, CLIPS + 1)
    rows = jax.vmap(lambda k: jax.random.permutation(k, TEXT)[:RECOMP])(keys[:CLIPS]).astype(jnp.int32)
    inner = (jax.random.permutation(keys[CLIPS], TEXT - 2)[:RECOMP - 2] + 1).astype(jnp.int32)
    first = jnp.concatenate([jnp.array([0, TEXT - 1], jnp.int32), inner])
    first = jax.random.permutation(jax.random.fold_in(key, 7), first).astype(jnp.int32)
    return rows.at[0].set(first)


def draw_clip_len(key, part):
    vals = jax.random.randint(key, (CLIPS,), LMAX // 4, LMAX + 1).astype(jnp.int32)
    order = jax.random.permutation(jax.random.fold_in(key, 1), CLIPS)
    return vals.at[order[0]].set(LMAX).at[order[1]].set(LMAX // 4).astype(jnp.int32)


def draw_text_len(key, part):
    vals = jax.random.randint(key, (CLIPS,), TEXT // 4, TEXT + 1).astype(jnp.int32)
    order = jax.random.permutation(jax.random.fold_in(key, 2), CLIPS)
    return vals.at[order[0]].set(TEXT).at[order[1]].set(TEXT // 4).astype(jnp.int32)


def steps_of(rng, shape, cuts, smallest, top_value):
    def one(position, shards_of):
        heights = jax.random.uniform(jax.random.fold_in(jax.random.fold_in(rng, 6), position), (shards_of,), jnp.float32, smallest / len(cuts), top_value / len(cuts))
        return jnp.repeat(jnp.exp(heights), shape[position] // shards_of).reshape((-1,) + (1,) * (len(shape) - position - 1))

    level = one(*cuts[0])
    for cut in cuts[1:]:
        level = level * one(*cut)
    return level


def normal_values(stream_key, shape, spread, most, pieces=(), held_as=jnp.bfloat16):
    values = spread * jax.random.normal(stream_key, shape, jnp.float32)
    if pieces:
        values = values * steps_of(stream_key, shape, pieces, -0.22, 0.18)
    return jnp.clip(values, -most, most).astype(held_as)


def setup_inputs(seed: int = 0) -> dict:
    key_of = jax.random.split(jax.random.key(seed), 13)
    hidden = normal_values(key_of[0], (CLIPS, LMAX, D), 1.0, 6.0, ((0, 4),))
    norm_gain = jnp.clip(jnp.exp(jax.random.uniform(key_of[1], (D,), jnp.float32, math.log(0.5), math.log(2.0))), 0.5, 2.0)
    q_weight = normal_values(key_of[2], (D, INNER), D ** -0.5, 0.078125, ((0, 32),), jnp.float32)
    k_weight = normal_values(key_of[3], (D, INNER), D ** -0.5, 0.078125, ((0, 32),), jnp.float32)
    v_weight = normal_values(key_of[4], (D, INNER), D ** -0.5, 0.078125, ((0, 32),), jnp.float32)
    o_weight = normal_values(key_of[5], (D, INNER), HD ** -0.5, 0.5, ((0, 32),), jnp.float32)
    key_cache = draw_key_cache(jax.random.fold_in(key_of[12], 71), 0)
    value_cache = normal_values(key_of[7], (CLIPS, TEXT, INNER), 1.0, 6.0, ((0, 4), (2, 8)))
    text_rows = normal_values(key_of[8], (CLIPS, RECOMP, D), 1.0, 6.0, ((0, 4), (1, 8)))
    text_index = draw_text_index(jax.random.fold_in(key_of[12], 71), 0)
    clip_len = draw_clip_len(jax.random.fold_in(key_of[12], 71), 0)
    text_len = draw_text_len(jax.random.fold_in(key_of[12], 71), 0)
    return dict(hidden=hidden, norm_gain=norm_gain, q_weight=q_weight, k_weight=k_weight, v_weight=v_weight, o_weight=o_weight, key_cache=key_cache, value_cache=value_cache, text_rows=text_rows, text_index=text_index, clip_len=clip_len, text_len=text_len)


def attend_clip(args):
    query, keys, values, live = args
    qh = query.astype(jnp.float32).reshape(LMAX, HEADS, HD)
    kh = keys.astype(jnp.float32).reshape(TEXT, HEADS, HD)
    vh = values.astype(jnp.float32).reshape(TEXT, HEADS, HD)
    score = jnp.einsum('lhe,jhe->hlj', qh, kh) * (1.0 / math.sqrt(HD))
    valid = jnp.arange(TEXT) < live
    score = jnp.where(valid[None, None, :], score, -1e+30)
    top = lax.optimization_barrier(jnp.max(score, axis=-1, keepdims=True))
    expo = jnp.exp(score - top)
    weights = (expo / lax.optimization_barrier(jnp.sum(expo, axis=-1, keepdims=True))).astype(jnp.bfloat16)
    attended = jnp.einsum('hlj,jhe->lhe', weights.astype(jnp.float32), vh)
    return attended.astype(jnp.bfloat16).reshape(LMAX, INNER)

def reference(hidden, norm_gain, q_weight, k_weight, v_weight, o_weight, key_cache, value_cache, text_rows, text_index, clip_len, text_len):
    wq = q_weight.astype(jnp.bfloat16)
    wk = k_weight.astype(jnp.bfloat16)
    wv = v_weight.astype(jnp.bfloat16)
    wo = o_weight.astype(jnp.bfloat16)
    x32 = hidden.astype(jnp.float32)
    mean = lax.optimization_barrier(jnp.mean(x32, axis=-1, keepdims=True))
    centered = x32 - mean
    var = lax.optimization_barrier(jnp.mean(centered * centered, axis=-1, keepdims=True))
    normed = (centered * lax.rsqrt(var + 1e-06) * norm_gain).astype(jnp.bfloat16)
    query = jnp.dot(normed.reshape(CLIPS * LMAX, D), wq, preferred_element_type=jnp.float32).astype(jnp.bfloat16).reshape(CLIPS, LMAX, INNER)
    flat_text = text_rows.reshape(CLIPS * RECOMP, D)
    new_keys = jnp.dot(flat_text, wk, preferred_element_type=jnp.float32).astype(jnp.bfloat16).reshape(CLIPS, RECOMP, INNER)
    new_values = jnp.dot(flat_text, wv, preferred_element_type=jnp.float32).astype(jnp.bfloat16).reshape(CLIPS, RECOMP, INNER)
    keys = jax.vmap(lambda cache, rows, fresh: cache.at[rows].set(fresh))(key_cache, text_index, new_keys)
    values = jax.vmap(lambda cache, rows, fresh: cache.at[rows].set(fresh))(value_cache, text_index, new_values)
    attended = lax.map(attend_clip, (query, keys, values, text_len))
    att_heads = attended.reshape(CLIPS * LMAX, HEADS, HD).transpose(1, 0, 2)
    wo_heads = wo.reshape(D, HEADS, HD).transpose(1, 0, 2)

    def add_head(total, pair):
        term = jnp.dot(pair[0], pair[1].T, preferred_element_type=jnp.float32)
        rounded = lax.optimization_barrier(term.astype(jnp.bfloat16))
        return (total + rounded.astype(jnp.float32), None)
    summed, _ = lax.scan(add_head, jnp.zeros((CLIPS * LMAX, D), jnp.float32), (att_heads, wo_heads))
    summed = summed.reshape(CLIPS, LMAX, D)
    live = jnp.arange(LMAX)[None, :] < clip_len[:, None]
    return (x32 + jnp.where(live[:, :, None], summed, 0.0)).astype(jnp.bfloat16)
```

```python
import functools
import math

import jax
import jax.numpy as jnp
from jax import lax
from jax.experimental import pallas as pl
from jax.experimental.pallas import tpu as pltpu
from jax.sharding import PartitionSpec as P


def on_device(
    hidden,
    norm_gain,
    q_weight,
    k_weight,
    v_weight,
    o_weight,
    key_cache,
    value_cache,
    text_rows,
    text_index,
    clip_len,
    text_len,
):
    head_width = key_cache.shape[2]
    text_total = key_cache.shape[1]
    q_half = q_weight.astype(jnp.bfloat16)
    k_half = k_weight.astype(jnp.bfloat16)
    v_half = v_weight.astype(jnp.bfloat16)
    o_half = o_weight.astype(jnp.bfloat16)
    q_block, k_block, v_block, o_block = (
        lax.all_to_all(q_half, "tp", split_axis=1, concat_axis=0, tiled=True),
        lax.all_to_all(k_half, "tp", split_axis=1, concat_axis=0, tiled=True),
        lax.all_to_all(v_half, "tp", split_axis=1, concat_axis=0, tiled=True),
        lax.all_to_all(o_half, "tp", split_axis=1, concat_axis=0, tiled=True),
    )
    q_local, k_local, v_local, o_local = (
        lax.all_gather(q_block, "req", axis=0, tiled=True),
        lax.all_gather(k_block, "req", axis=0, tiled=True),
        lax.all_gather(v_block, "req", axis=0, tiled=True),
        lax.all_gather(o_block, "req", axis=0, tiled=True),
    )
    x32 = hidden[0].astype(jnp.float32)
    mean = jnp.mean(x32, axis=-1, keepdims=True)
    centered = x32 - mean
    var = jnp.mean(centered * centered, axis=-1, keepdims=True)
    normed = (centered * lax.rsqrt(var + 1e-06) * norm_gain).astype(jnp.bfloat16)
    kv_local = jnp.concatenate([k_local, v_local], axis=1)
    new_kv = jnp.einsum(
        "crd,de->cre",
        lax.all_gather(text_rows, "tp", axis=1, tiled=True),
        kv_local,
        preferred_element_type=jnp.float32,
    ).astype(jnp.bfloat16)
    query = jnp.dot(normed, q_local, preferred_element_type=jnp.float32).astype(jnp.bfloat16)
    selector = text_index[0][None, :] == jnp.arange(text_total, dtype=jnp.int32)[:, None]
    covered = jnp.any(selector, axis=1)
    placed = jnp.dot(
        selector.astype(jnp.bfloat16), new_kv[0], preferred_element_type=jnp.float32
    ).astype(jnp.bfloat16)
    keys = jnp.where(covered[:, None], placed[:, :head_width], key_cache[0])
    values = jnp.where(covered[:, None], placed[:, head_width:], value_cache[0])
    score = lax.dot_general(
        query, keys, (((1,), (1,)), ((), ())), preferred_element_type=jnp.float32
    ) * (1.0 / math.sqrt(head_width))
    valid = jnp.arange(text_total, dtype=jnp.int32) < text_len[0]
    score = jnp.where(valid[None, :], score, -1e30)
    top = jnp.max(score, axis=-1, keepdims=True)
    expo = jnp.exp(score - top)
    weights = (expo / jnp.sum(expo, axis=-1, keepdims=True)).astype(jnp.bfloat16)
    attended = jnp.dot(weights, values, preferred_element_type=jnp.float32).astype(jnp.bfloat16)
    tp_count = lax.axis_size("tp")
    local_rows = hidden.shape[1] // tp_count
    first_row = lax.axis_index("tp") * local_rows
    summed = lax.psum_scatter(
        lax.dot_general(
            attended, o_local, (((1,), (1,)), ((), ())), preferred_element_type=jnp.float32
        ).astype(jnp.bfloat16),
        "tp",
        scatter_dimension=0,
        tiled=True,
    ).astype(jnp.float32)
    own_rows = lax.dynamic_slice_in_dim(x32, first_row, local_rows, 0)
    positions = first_row + jnp.arange(local_rows, dtype=jnp.int32)
    live = positions < clip_len[0]
    result = own_rows + jnp.where(live[:, None], summed, 0.0)
    return result.astype(jnp.bfloat16)[None]


MESH = pl.DeviceIdType.MESH
BF16 = jnp.bfloat16
F32 = jnp.float32


def flip(index, mask):
    result = 0
    for bit in (1, 2, 4):
        has = (index // bit) % 2
        result = result + bit * ((1 - has) if mask & bit else has)
    return result


def fused_kernel(
    hidden,
    gain,
    qw,
    kw,
    vw,
    ow,
    kc,
    vc,
    text,
    tidx,
    clen,
    tlen,
    out,
    wsend,
    wall,
    tall,
    oall,
    normed,
    resid,
    att,
    ftot,
    fsend,
    frecv,
    w_ss,
    w_rs,
    x_ss,
    t_ss,
    t_rs,
    o_ss,
    o_rs,
    a_ss,
    a_rs,
    f_ss,
    f_rs,
):
    slots, width = hidden.shape
    block = qw.shape[0]
    text_total, hd = kc.shape
    r = lax.axis_index("req")
    t = lax.axis_index("tp")
    z, y = t // 2, t % 2
    r1 = r + 1 - 2 * (r % 2)
    r2 = (r + 2) % 4
    r3 = (r1 + 2) % 4
    me = r * 8 + t

    def send(src, dst, ss, rs, **dev):
        return pltpu.make_async_remote_copy(
            src_ref=src, dst_ref=dst, send_sem=ss, recv_sem=rs, device_id=dev, device_id_type=MESH
        )

    barrier = pltpu.get_barrier_semaphore()
    for i in range(1, 8):
        pl.semaphore_signal(barrier, inc=1, device_id={"tp": flip(t, i)}, device_id_type=MESH)
    for peer in (r1, r2):
        pl.semaphore_signal(barrier, inc=1, device_id={"req": peer}, device_id_type=MESH)

    tall[t] = text[...]
    for h in range(8):
        cols = slice(h * hd, (h + 1) * hd)
        wsend[h] = jnp.concatenate(
            [qw[:, cols].astype(BF16), kw[:, cols].astype(BF16), vw[:, cols].astype(BF16)], axis=1
        )
    wall[me] = wsend[t]
    oall[r] = ow[...].astype(BF16)
    pl.semaphore_wait(barrier, 9)

    def text_copy(shard, way, sem):
        slot = 2 * shard + y
        if way == 0:
            target = 2 * z + 1 - y
        else:
            target = 2 * (z + way) + y
        return send(tall.at[slot], tall.at[slot], t_ss.at[sem], t_rs.at[slot], tp=target)

    def text_step(d, wait_send=False):
        for side in (1, -1):
            if d == 0 and side == -1:
                continue
            shard = z - side * d
            inside = (shard >= 0) & (shard <= 3)
            base = 3 * (2 * d + (side < 0))

            @pl.when(inside)
            def _():
                if d > 0 and not wait_send:
                    text_copy(shard, 0, base).wait_recv()
                across = text_copy(shard, 0, base)
                if wait_send:
                    across.wait_send()
                else:
                    across.start()
                for way in (1, -1):
                    if d > 0 and way != side:
                        continue
                    onward = text_copy(shard, way, base + (1 if way == 1 else 2))

                    @pl.when((z + way >= 0) & (z + way <= 3))
                    def _():
                        if wait_send:
                            onward.wait_send()
                        else:
                            onward.start()

    text_step(0)

    o_copies = [
        send(oall.at[r], oall.at[r], o_ss.at[0], o_rs.at[r], req=r1),
        send(oall.at[r], oall.at[r], o_ss.at[1], o_rs.at[r], req=r2),
        send(oall.at[r2], oall.at[r2], o_ss.at[2], o_rs.at[r2], req=r1),
    ]
    w_copies = [
        send(wsend.at[flip(t, i)], wall.at[me], w_ss.at[i], w_rs.at[me], tp=flip(t, i))
        for i in range(1, 8)
    ]

    def onward(i, which):
        if which == 2:
            slot, target = r2 * 8 + flip(t, i), r1
        else:
            slot, target = r * 8 + flip(t, i), (r1 if which == 0 else r2)
        return send(wall.at[slot], wall.at[slot], x_ss.at[8 * which + i], w_rs.at[slot], req=target)

    def w_arrived(owner, i):
        slot = owner * 8 + flip(t, i)
        send(wall.at[slot], wall.at[slot], w_ss.at[0], w_rs.at[slot], req=r1).wait_recv()

    def o_arrived(owner):
        send(oall.at[owner], oall.at[owner], o_ss.at[0], o_rs.at[owner], req=r1).wait_recv()

    for copy in w_copies:
        copy.start()
    onward(0, 1).start()
    onward(0, 0).start()
    o_copies[1].start()
    o_copies[0].start()

    def norm_rows(c, carry):
        rows = pl.ds(pl.multiple_of(c * 16, 16), 16)
        x = hidden[rows, :].astype(F32)
        mean = jnp.mean(x, axis=-1, keepdims=True)
        centered = x - mean
        var = jnp.mean(centered * centered, axis=-1, keepdims=True)
        normed[rows, :] = (centered * lax.rsqrt(var + 1e-06) * gain[...]).astype(BF16)
        return carry

    lax.fori_loop(0, slots // 16, norm_rows, 0)

    text_step(1)
    for i in (1, 2, 3):
        w_arrived(r, i)
        onward(i, 1).start()
        onward(i, 0).start()
    text_step(2)
    for i in (4, 5, 6, 7):
        w_arrived(r, i)
        onward(i, 1).start()
        onward(i, 0).start()
    text_step(3)

    span = 8 * block
    picked = (
        lax.broadcasted_iota(jnp.int32, (span, block), 0)
        == lax.broadcasted_iota(jnp.int32, (span, block), 1) + t * block
    )
    pick = jnp.where(picked, 1.0, 0.0).astype(BF16)
    resid[...] = jnp.concatenate(
        [
            jnp.dot(hidden[:, g * span : (g + 1) * span], pick, preferred_element_type=F32)
            for g in range(4)
        ],
        axis=1,
    )

    for i in range(8):
        w_arrived(r2, i)
        onward(i, 2).start()
    o_arrived(r2)
    o_copies[2].start()
    for i in range(8):
        w_arrived(r1, i)
    for i in range(8):
        w_arrived(r3, i)
    for shard in range(4):
        slot = 2 * shard + 1 - y
        send(tall.at[slot], tall.at[slot], t_ss.at[0], t_rs.at[slot], tp=flip(t, 1)).wait_recv()

    query = jnp.zeros((slots, hd), F32)
    fresh = jnp.zeros((8 * text.shape[0], 2 * hd), F32)
    for g in range(4):
        cols = slice(g * span, (g + 1) * span)
        part = slice(8 * g, 8 * g + 8)
        query += jnp.dot(
            normed[:, cols],
            wall[part, :, 0:hd].reshape(span, hd),
            preferred_element_type=F32,
        )
        fresh += jnp.dot(
            tall[:, :, cols].reshape(8 * text.shape[0], span),
            wall[part, :, hd : 3 * hd].reshape(span, 2 * hd),
            preferred_element_type=F32,
        )
    query = query.astype(BF16)
    fresh = fresh.astype(BF16)

    recomp = tidx.shape[1]
    row = lax.broadcasted_iota(jnp.int32, (text_total, recomp), 0)
    selector = jnp.where(tidx[...] == row, 1.0, 0.0)
    covered = jnp.sum(selector, axis=1, keepdims=True) > 0.5
    placed = jnp.dot(selector.astype(BF16), fresh, preferred_element_type=F32)
    keys = jnp.where(covered, placed[:, :hd], kc[...].astype(F32)).astype(BF16)
    values = jnp.where(covered, placed[:, hd:], vc[...].astype(F32)).astype(BF16)
    score = lax.dot_general(query, keys, (((1,), (1,)), ((), ())), preferred_element_type=F32)
    score = score * (1.0 / math.sqrt(hd))
    column = lax.broadcasted_iota(jnp.int32, score.shape, 1)
    score = jnp.where(column < tlen[0], score, -1e30)
    top = jnp.max(score, axis=-1, keepdims=True)
    expo = jnp.exp(score - top)
    weights = (expo / jnp.sum(expo, axis=-1, keepdims=True)).astype(BF16)
    att[t] = jnp.dot(weights, values, preferred_element_type=F32).astype(BF16)

    a_copies = [
        send(att.at[t], att.at[t], a_ss.at[i], a_rs.at[t], tp=flip(t, i)) for i in range(1, 8)
    ]
    for copy in a_copies:
        copy.start()
    o_arrived(r1)
    o_arrived(r3)
    for i in range(1, 8):
        slot = flip(t, i)
        send(att.at[slot], att.at[slot], a_ss.at[0], a_rs.at[slot], tp=slot).wait_recv()

    step = 80
    for c in range(slots // step):
        total = jnp.zeros((step, 4 * block), F32)
        for h in range(8):
            term = lax.dot_general(
                att[h, c * step : (c + 1) * step, :],
                oall[:, :, h * hd : (h + 1) * hd].reshape(4 * block, hd),
                (((1,), (1,)), ((), ())),
                preferred_element_type=F32,
            )
            total += term.astype(BF16).astype(F32)
        position = lax.broadcasted_iota(jnp.int32, total.shape, 0) + c * step
        rows = slice(c * step, (c + 1) * step)
        ftot[rows, :] = resid[rows, :] + jnp.where(position < clen[0], total, 0.0)
    local = slots // 8
    padded = fsend.shape[1]
    ftot[slots : slots + padded - local, :] = jnp.zeros((padded - local, 4 * block), F32)
    for j in range(8):
        fsend[j] = ftot[j * local : j * local + padded, :].astype(BF16)
    f_copies = [
        send(fsend.at[flip(t, i)], frecv.at[t], f_ss.at[i], f_rs.at[t], tp=flip(t, i))
        for i in range(1, 8)
    ]
    for copy in f_copies:
        copy.start()
    frecv[t] = fsend[t]
    for i in range(1, 8):
        slot = flip(t, i)
        send(frecv.at[slot], frecv.at[slot], f_ss.at[0], f_rs.at[slot], tp=slot).wait_recv()
    for g in range(4):
        pieces = [
            frecv[j].astype(F32)[:local, g * block : (g + 1) * block] for j in range(8)
        ]
        out[:, g * span : (g + 1) * span] = jnp.concatenate(pieces, axis=1).astype(BF16)

    for d in range(4):
        text_step(d, wait_send=True)
    for copy in w_copies + o_copies + a_copies + f_copies:
        copy.wait_send()
    for which in range(3):
        for i in range(8):
            onward(i, which).wait_send()


def fused(hidden, gain, qw, kw, vw, ow, kc, vc, text, tidx, clen, tlen):
    _, slots, width = hidden.shape
    block, inner = qw.shape
    _, text_total, hd = kc.shape
    local = slots // 8
    padded = -(-local // 16) * 16
    vmem = pl.BlockSpec(memory_space=pltpu.VMEM)
    smem = pl.BlockSpec(memory_space=pltpu.SMEM)
    dma = pltpu.SemaphoreType.DMA
    result = pl.pallas_call(
        fused_kernel,
        out_shape=jax.ShapeDtypeStruct((local, width), BF16),
        in_specs=[vmem] * 10 + [smem] * 2,
        out_specs=vmem,
        scratch_shapes=[
            pltpu.VMEM((8, block, 3 * hd), BF16),
            pltpu.VMEM((32, block, 3 * hd), BF16),
            pltpu.VMEM((8, text.shape[1], width), BF16),
            pltpu.VMEM((4, block, inner), BF16),
            pltpu.VMEM((slots, width), BF16),
            pltpu.VMEM((slots, 4 * block), F32),
            pltpu.VMEM((8, slots, hd), BF16),
            pltpu.VMEM((slots + padded - local, 4 * block), F32),
            pltpu.VMEM((8, padded, 4 * block), BF16),
            pltpu.VMEM((8, padded, 4 * block), BF16),
            dma((8,)),
            dma((32,)),
            dma((24,)),
            dma((24,)),
            dma((8,)),
            dma((3,)),
            dma((4,)),
            dma((8,)),
            dma((8,)),
            dma((8,)),
            dma((8,)),
        ],
        compiler_params=pltpu.CompilerParams(
            collective_id=0, has_side_effects=True, vmem_limit_bytes=56 * 1024 * 1024
        ),
        cost_estimate=pl.CostEstimate(
            flops=3 * 10**9, bytes_accessed=10**7, transcendentals=slots * text_total
        ),
    )(
        hidden[0], gain[None], qw, kw, vw, ow, kc[0], vc[0], text[0], tidx, clen, tlen
    )
    return result[None]


def solution(mesh):
    def run(*args):
        hidden, qw, text = args[0], args[2], args[8]
        fits = (
            (mesh.shape["req"], mesh.shape["tp"]) == (4, 8)
            and qw.shape[0] % 16 == 0
            and text.shape[1] % 16 == 0
            and hidden.shape[1] % 80 == 0
        )
        return (fused if fits else on_device)(*args)

    return jax.shard_map(
        run,
        mesh=mesh,
        in_specs=(
            P("req", None, None),
            P(),
            P(("req", "tp"), None),
            P(("req", "tp"), None),
            P(("req", "tp"), None),
            P(("req", "tp"), None),
            P("req", None, "tp"),
            P("req", None, "tp"),
            P("req", "tp", None),
            P("req", None),
            P("req"),
            P("req"),
        ),
        out_specs=P("req", "tp", None),
        check_vma=False,
    )
```

```python
import functools
import math

import jax
import jax.numpy as jnp
from jax import lax
from jax.experimental import pallas as pl
from jax.experimental.pallas import tpu as pltpu
from jax.sharding import PartitionSpec as P


def on_device(
    hidden,
    norm_gain,
    q_weight,
    k_weight,
    v_weight,
    o_weight,
    key_cache,
    value_cache,
    text_rows,
    text_index,
    clip_len,
    text_len,
):
    head_width = key_cache.shape[2]
    text_total = key_cache.shape[1]
    q_half = q_weight.astype(jnp.bfloat16)
    k_half = k_weight.astype(jnp.bfloat16)
    v_half = v_weight.astype(jnp.bfloat16)
    o_half = o_weight.astype(jnp.bfloat16)
    q_block, k_block, v_block, o_block = (
        lax.all_to_all(q_half, "tp", split_axis=1, concat_axis=0, tiled=True),
        lax.all_to_all(k_half, "tp", split_axis=1, concat_axis=0, tiled=True),
        lax.all_to_all(v_half, "tp", split_axis=1, concat_axis=0, tiled=True),
        lax.all_to_all(o_half, "tp", split_axis=1, concat_axis=0, tiled=True),
    )
    q_local, k_local, v_local, o_local = (
        lax.all_gather(q_block, "req", axis=0, tiled=True),
        lax.all_gather(k_block, "req", axis=0, tiled=True),
        lax.all_gather(v_block, "req", axis=0, tiled=True),
        lax.all_gather(o_block, "req", axis=0, tiled=True),
    )
    x32 = hidden[0].astype(jnp.float32)
    mean = jnp.mean(x32, axis=-1, keepdims=True)
    centered = x32 - mean
    var = jnp.mean(centered * centered, axis=-1, keepdims=True)
    normed = (centered * lax.rsqrt(var + 1e-06) * norm_gain).astype(jnp.bfloat16)
    kv_local = jnp.concatenate([k_local, v_local], axis=1)
    new_kv = jnp.einsum(
        "crd,de->cre",
        lax.all_gather(text_rows, "tp", axis=1, tiled=True),
        kv_local,
        preferred_element_type=jnp.float32,
    ).astype(jnp.bfloat16)
    query = jnp.dot(normed, q_local, preferred_element_type=jnp.float32).astype(jnp.bfloat16)
    selector = text_index[0][None, :] == jnp.arange(text_total, dtype=jnp.int32)[:, None]
    covered = jnp.any(selector, axis=1)
    placed = jnp.dot(
        selector.astype(jnp.bfloat16), new_kv[0], preferred_element_type=jnp.float32
    ).astype(jnp.bfloat16)
    keys = jnp.where(covered[:, None], placed[:, :head_width], key_cache[0])
    values = jnp.where(covered[:, None], placed[:, head_width:], value_cache[0])
    score = lax.dot_general(
        query, keys, (((1,), (1,)), ((), ())), preferred_element_type=jnp.float32
    ) * (1.0 / math.sqrt(head_width))
    valid = jnp.arange(text_total, dtype=jnp.int32) < text_len[0]
    score = jnp.where(valid[None, :], score, -1e30)
    top = jnp.max(score, axis=-1, keepdims=True)
    expo = jnp.exp(score - top)
    weights = (expo / jnp.sum(expo, axis=-1, keepdims=True)).astype(jnp.bfloat16)
    attended = jnp.dot(weights, values, preferred_element_type=jnp.float32).astype(jnp.bfloat16)
    tp_count = lax.axis_size("tp")
    local_rows = hidden.shape[1] // tp_count
    first_row = lax.axis_index("tp") * local_rows
    summed = lax.psum_scatter(
        lax.dot_general(
            attended, o_local, (((1,), (1,)), ((), ())), preferred_element_type=jnp.float32
        ).astype(jnp.bfloat16),
        "tp",
        scatter_dimension=0,
        tiled=True,
    ).astype(jnp.float32)
    own_rows = lax.dynamic_slice_in_dim(x32, first_row, local_rows, 0)
    positions = first_row + jnp.arange(local_rows, dtype=jnp.int32)
    live = positions < clip_len[0]
    result = own_rows + jnp.where(live[:, None], summed, 0.0)
    return result.astype(jnp.bfloat16)[None]


MESH = pl.DeviceIdType.MESH
BF16 = jnp.bfloat16
F32 = jnp.float32


def flip(index, mask):
    result = 0
    for bit in (1, 2, 4):
        has = (index // bit) % 2
        result = result + bit * ((1 - has) if mask & bit else has)
    return result


def fused_kernel(
    hidden_hbm,
    gain,
    qw,
    kw,
    vw,
    ow,
    kc,
    vc,
    text,
    tidx,
    clen,
    tlen,
    out,
    hidden,
    freshbuf,
    selector,
    covering,
    wsend,
    wall,
    tall,
    oall,
    normed,
    resid,
    att,
    ftot,
    fsend,
    frecv,
    w_ss,
    w_rs,
    x_ss,
    t_ss,
    t_rs,
    o_ss,
    o_rs,
    a_ss,
    a_rs,
    f_ss,
    f_rs,
    h_sem,
):
    slots, width = hidden.shape
    block = qw.shape[0]
    text_total, hd = kc.shape
    r = lax.axis_index("req")
    t = lax.axis_index("tp")
    z, y = t // 2, t % 2
    r1 = r + 1 - 2 * (r % 2)
    r2 = (r + 2) % 4
    r3 = (r1 + 2) % 4
    me = r * 8 + t

    def send(src, dst, ss, rs, **dev):
        return pltpu.make_async_remote_copy(
            src_ref=src, dst_ref=dst, send_sem=ss, recv_sem=rs, device_id=dev, device_id_type=MESH
        )

    barrier = pltpu.get_barrier_semaphore()
    for i in range(1, 8):
        pl.semaphore_signal(barrier, inc=1, device_id={"tp": flip(t, i)}, device_id_type=MESH)
    for peer in (r1, r2):
        pl.semaphore_signal(barrier, inc=1, device_id={"req": peer}, device_id_type=MESH)

    hidden_copy = pltpu.make_async_copy(hidden_hbm, hidden, h_sem)
    hidden_copy.start()
    tall[y, z] = text[...]
    for h in range(8):
        cols = slice(h * hd, (h + 1) * hd)
        wsend[h] = jnp.concatenate(
            [qw[:, cols].astype(BF16), kw[:, cols].astype(BF16), vw[:, cols].astype(BF16)], axis=1
        )
    wall[me] = wsend[t]
    oall[r] = ow[...].astype(BF16)
    pl.semaphore_wait(barrier, 9)

    def chain_copy(ref, ss, rs, part, shard, way, sem):
        target = 2 * z + 1 - y if way == 0 else 2 * (z + way) + y
        piece = ref(y, shard, part)
        slot = rs.shape[0] // 8 * (4 * y + shard) + part
        return send(piece, piece, ss.at[sem], rs.at[slot], tp=target)

    def chain_step(ref, ss, rs, part, d, wait_send=False, then=None):
        parts = rs.shape[0] // 8
        for side in (1, -1):
            if d == 0 and side == -1:
                continue
            shard = z - side * d
            base = 3 * (parts * (2 * d + (side < 0)) + part)

            @pl.when((shard >= 0) & (shard <= 3))
            def _():
                across = chain_copy(ref, ss, rs, part, shard, 0, base)
                if d > 0 and not wait_send:
                    across.wait_recv()
                for way in (1, -1):
                    if d > 0 and way != side:
                        continue
                    onward = chain_copy(
                        ref, ss, rs, part, shard, way, base + (1 if way == 1 else 2)
                    )

                    @pl.when((z + way >= 0) & (z + way <= 3))
                    def _():
                        if wait_send:
                            onward.wait_send()
                        else:
                            onward.start()

                if wait_send:
                    across.wait_send()
                else:
                    across.start()
                if then is not None:
                    then(y, shard)

    def crossed(ref, ss, rs, part, shard):
        piece = ref(1 - y, shard, part)
        slot = rs.shape[0] // 8 * (4 * (1 - y) + shard) + part
        send(piece, piece, ss.at[0], rs.at[slot], tp=flip(t, 1)).wait_recv()

    def text_ref(column, shard, part):
        return tall.at[column, shard, part]

    def att_ref(column, shard, part):
        return att.at[2 * shard + column]

    def text_step(d, wait_send=False):
        for part in range(2):
            chain_step(text_ref, t_ss, t_rs, part, d, wait_send)

    text_step(0)

    o_copies = [
        send(oall.at[r], oall.at[r], o_ss.at[0], o_rs.at[r], req=r1),
        send(oall.at[r], oall.at[r], o_ss.at[1], o_rs.at[r], req=r2),
        send(oall.at[r2], oall.at[r2], o_ss.at[2], o_rs.at[r2], req=r1),
    ]
    w_copies = [
        send(wsend.at[flip(t, i)], wall.at[me], w_ss.at[i], w_rs.at[me], tp=flip(t, i))
        for i in range(1, 8)
    ]

    def onward(i, which):
        if which == 2:
            slot, target = r2 * 8 + flip(t, i), r1
        else:
            slot, target = r * 8 + flip(t, i), (r1 if which == 0 else r2)
        return send(wall.at[slot], wall.at[slot], x_ss.at[8 * which + i], w_rs.at[slot], req=target)

    def w_arrived(owner, i):
        slot = owner * 8 + flip(t, i)
        send(wall.at[slot], wall.at[slot], w_ss.at[0], w_rs.at[slot], req=r1).wait_recv()

    def o_arrived(owner):
        send(oall.at[owner], oall.at[owner], o_ss.at[0], o_rs.at[owner], req=r1).wait_recv()

    for copy in w_copies:
        copy.start()
    onward(0, 1).start()
    onward(0, 0).start()
    o_copies[1].start()
    o_copies[0].start()

    def norm_rows(c, carry):
        rows = pl.ds(pl.multiple_of(c * 16, 16), 16)
        x = hidden[rows, :].astype(F32)
        mean = jnp.mean(x, axis=-1, keepdims=True)
        centered = x - mean
        var = jnp.mean(centered * centered, axis=-1, keepdims=True)
        normed[rows, :] = (centered * lax.rsqrt(var + 1e-06) * gain[...]).astype(BF16)
        return carry

    hidden_copy.wait()
    lax.fori_loop(0, slots // 16, norm_rows, 0)

    text_step(1)
    for i in (1, 2, 3):
        w_arrived(r, i)
        onward(i, 1).start()
        onward(i, 0).start()
    text_step(2)
    for i in (4, 5, 6, 7):
        w_arrived(r, i)
        onward(i, 1).start()
        onward(i, 0).start()
    text_step(3)

    span = 8 * block
    picked = (
        lax.broadcasted_iota(jnp.int32, (span, block), 0)
        == lax.broadcasted_iota(jnp.int32, (span, block), 1) + t * block
    )
    pick = jnp.where(picked, 1.0, 0.0).astype(BF16)
    resid[...] = jnp.concatenate(
        [
            jnp.dot(hidden[:, g * span : (g + 1) * span], pick, preferred_element_type=F32)
            for g in range(4)
        ],
        axis=1,
    )
    recomp = tidx.shape[1]
    row = lax.broadcasted_iota(jnp.int32, (text_total, recomp), 0)
    chosen = jnp.where(tidx[...] == row, 1.0, 0.0)
    selector[...] = chosen.astype(BF16)
    covering[...] = jnp.broadcast_to(jnp.sum(chosen, axis=1, keepdims=True), covering.shape)

    def query_part(g):
        return jnp.dot(
            normed[:, pl.ds(pl.multiple_of(g * span, span), span)],
            wall[pl.ds(8 * g, 8), :, 0:hd].reshape(span, hd),
            preferred_element_type=F32,
        )

    for i in range(8):
        w_arrived(r2, i)
        onward(i, 2).start()
    o_arrived(r2)
    o_copies[2].start()
    query = query_part(r) + query_part(r2)
    for i in range(8):
        w_arrived(r1, i)
    query += query_part(r1)
    for i in range(8):
        w_arrived(r3, i)
    query += query_part(r3)
    query = query.astype(BF16)

    shard_rows = text.shape[0] * text.shape[1]

    def fresh_rows(column):
        lines = tall[column].reshape(4 * shard_rows, 4 * span)
        part = jnp.dot(
            lines, wall[:, :, hd : 3 * hd].reshape(4 * span, 2 * hd), preferred_element_type=F32
        ).astype(BF16)
        for shard in range(4):
            freshbuf[2 * shard + column] = part[shard * shard_rows : (shard + 1) * shard_rows]

    fresh_rows(y)
    for shard in range(4):
        for part in range(2):
            crossed(text_ref, t_ss, t_rs, part, shard)
    fresh_rows(1 - y)
    fresh = freshbuf[...].reshape(recomp, 2 * hd)

    covered = covering[...] > 0.5
    placed = jnp.dot(selector[...], fresh, preferred_element_type=F32)
    keys = jnp.where(covered, placed[:, :hd], kc[...].astype(F32)).astype(BF16)
    values = jnp.where(covered, placed[:, hd:], vc[...].astype(F32)).astype(BF16)
    score = lax.dot_general(query, keys, (((1,), (1,)), ((), ())), preferred_element_type=F32)
    score = score * (1.0 / math.sqrt(hd))
    column = lax.broadcasted_iota(jnp.int32, score.shape, 1)
    score = jnp.where(column < tlen[0], score, -1e30)
    top = jnp.max(score, axis=-1, keepdims=True)
    expo = jnp.exp(score - top)
    weights = (expo / jnp.sum(expo, axis=-1, keepdims=True)).astype(BF16)
    att[t] = jnp.dot(weights, values, preferred_element_type=F32).astype(BF16)

    chain_step(att_ref, a_ss, a_rs, 0, 0)
    o_arrived(r1)
    o_arrived(r3)
    local = slots // 8
    step = 2 * local
    features = 4 * block

    def head_rows(slot, c):
        rows = pl.ds(pl.multiple_of(c * step, 16), step)
        head = pl.ds(pl.multiple_of(slot * hd, hd), hd)
        term = lax.dot_general(
            att[slot, rows, :],
            oall[:, :, head].reshape(features, hd),
            (((1,), (1,)), ((), ())),
            preferred_element_type=F32,
        )
        return rows, term.astype(BF16).astype(F32)

    def add_head(column, shard):
        def body(c, carry):
            rows, term = head_rows(2 * shard + column, c)
            ftot[rows, :] += term
            return carry

        lax.fori_loop(0, 4, body, 0)

    ftot[...] = jnp.zeros_like(ftot)
    add_head(y, z)
    for d in (1, 2, 3):
        chain_step(att_ref, a_ss, a_rs, 0, d, then=add_head)

    def z_flip(mask):
        return flip(t, 2 * mask) // 2

    for m in (0, 1, 3, 2):
        crossed(att_ref, a_ss, a_rs, 0, z_flip(m))
        if m != 2:
            add_head(1 - y, z_flip(m))

    tiles = features // 128
    padded = fsend.shape[1]
    f_copies = []
    for m in (3, 2, 1, 0):
        c = z_flip(m)
        rows, term = head_rows(2 * z_flip(2) + 1 - y, c)
        total = ftot[rows, :] + term
        position = lax.broadcasted_iota(jnp.int32, total.shape, 0) + c * step
        total = resid[rows, :] + jnp.where(position < clen[0], total, 0.0)
        for half in range(2):
            own = total[half * local : (half + 1) * local]
            pieces = [own[:, k * 128 : (k + 1) * 128] for k in range(tiles)]
            if padded > tiles * local:
                pieces.append(jnp.zeros((padded - tiles * local, 128), F32))
            fsend[2 * c + half] = jnp.concatenate(pieces, axis=0).astype(BF16)
        for i in (2 * m, 2 * m + 1):
            if i > 0:
                copy = send(
                    fsend.at[flip(t, i)], frecv.at[t], f_ss.at[i], f_rs.at[t], tp=flip(t, i)
                )
                copy.start()
                f_copies.append(copy)
    frecv[t] = fsend[t]
    for i in range(1, 8):
        slot = flip(t, i)
        send(frecv.at[slot], frecv.at[slot], f_ss.at[0], f_rs.at[slot], tp=slot).wait_recv()
    lines = []
    for j in range(8):
        got = frecv[j].astype(F32)
        lines.append(
            jnp.concatenate([got[k * local : (k + 1) * local] for k in range(tiles)], axis=1)
        )
    for g in range(4):
        pieces = [line[:, g * block : (g + 1) * block] for line in lines]
        out[:, g * span : (g + 1) * span] = jnp.concatenate(pieces, axis=1).astype(BF16)

    for d in range(4):
        text_step(d, wait_send=True)
        chain_step(att_ref, a_ss, a_rs, 0, d, wait_send=True)
    for copy in w_copies + o_copies + f_copies:
        copy.wait_send()
    for which in range(3):
        for i in range(8):
            onward(i, which).wait_send()


def fused(hidden, gain, qw, kw, vw, ow, kc, vc, text, tidx, clen, tlen):
    _, slots, width = hidden.shape
    block, inner = qw.shape
    _, text_total, hd = kc.shape
    local = slots // 8
    tiles = 4 * block // 128
    padded = -(-tiles * local // 16) * 16
    pieces = text[0].reshape(2, text.shape[1] // 2, width)
    vmem = pl.BlockSpec(memory_space=pltpu.VMEM)
    smem = pl.BlockSpec(memory_space=pltpu.SMEM)
    dma = pltpu.SemaphoreType.DMA
    result = pl.pallas_call(
        fused_kernel,
        out_shape=jax.ShapeDtypeStruct((local, width), BF16),
        in_specs=[pl.BlockSpec(memory_space=pltpu.HBM)] + [vmem] * 9 + [smem] * 2,
        out_specs=vmem,
        scratch_shapes=[
            pltpu.VMEM((slots, width), BF16),
            pltpu.VMEM((8, text.shape[1], 2 * hd), BF16),
            pltpu.VMEM((text_total, tidx.shape[1]), BF16),
            pltpu.VMEM((text_total, hd), F32),
            pltpu.VMEM((8, block, 3 * hd), BF16),
            pltpu.VMEM((32, block, 3 * hd), BF16),
            pltpu.VMEM((2, 4, *pieces.shape), BF16),
            pltpu.VMEM((4, block, inner), BF16),
            pltpu.VMEM((slots, width), BF16),
            pltpu.VMEM((slots, 4 * block), F32),
            pltpu.VMEM((8, slots, hd), BF16),
            pltpu.VMEM((slots, 4 * block), F32),
            pltpu.VMEM((8, padded, 128), BF16),
            pltpu.VMEM((8, padded, 128), BF16),
            dma((8,)),
            dma((32,)),
            dma((24,)),
            dma((48,)),
            dma((16,)),
            dma((3,)),
            dma((4,)),
            dma((24,)),
            dma((8,)),
            dma((8,)),
            dma((8,)),
            dma(()),
        ],
        compiler_params=pltpu.CompilerParams(
            collective_id=0, has_side_effects=True, vmem_limit_bytes=56 * 1024 * 1024
        ),
        cost_estimate=pl.CostEstimate(
            flops=3 * 10**9, bytes_accessed=10**7, transcendentals=slots * text_total
        ),
    )(
        hidden[0], gain[None], qw, kw, vw, ow, kc[0], vc[0], pieces, tidx, clen, tlen
    )
    return result[None]


def solution(mesh):
    def run(*args):
        hidden, qw, text = args[0], args[2], args[8]
        fits = (
            (mesh.shape["req"], mesh.shape["tp"]) == (4, 8)
            and qw.shape[0] % 16 == 0
            and text.shape[1] % 32 == 0
            and qw.shape[0] % 32 == 0
            and hidden.shape[1] % 80 == 0
        )
        return (fused if fits else on_device)(*args)

    return jax.shard_map(
        run,
        mesh=mesh,
        in_specs=(
            P("req", None, None),
            P(),
            P(("req", "tp"), None),
            P(("req", "tp"), None),
            P(("req", "tp"), None),
            P(("req", "tp"), None),
            P("req", None, "tp"),
            P("req", None, "tp"),
            P("req", "tp", None),
            P("req", None),
            P("req"),
            P("req"),
        ),
        out_specs=P("req", "tp", None),
        check_vma=False,
    )
```

```python
import functools
import math

import jax
import jax.numpy as jnp
from jax import lax
from jax.experimental import pallas as pl
from jax.experimental.pallas import tpu as pltpu
from jax.sharding import PartitionSpec as P


def on_device(
    hidden,
    norm_gain,
    q_weight,
    k_weight,
    v_weight,
    o_weight,
    key_cache,
    value_cache,
    text_rows,
    text_index,
    clip_len,
    text_len,
):
    head_width = key_cache.shape[2]
    text_total = key_cache.shape[1]
    q_half = q_weight.astype(jnp.bfloat16)
    k_half = k_weight.astype(jnp.bfloat16)
    v_half = v_weight.astype(jnp.bfloat16)
    o_half = o_weight.astype(jnp.bfloat16)
    q_block, k_block, v_block, o_block = (
        lax.all_to_all(q_half, "tp", split_axis=1, concat_axis=0, tiled=True),
        lax.all_to_all(k_half, "tp", split_axis=1, concat_axis=0, tiled=True),
        lax.all_to_all(v_half, "tp", split_axis=1, concat_axis=0, tiled=True),
        lax.all_to_all(o_half, "tp", split_axis=1, concat_axis=0, tiled=True),
    )
    q_local, k_local, v_local, o_local = (
        lax.all_gather(q_block, "req", axis=0, tiled=True),
        lax.all_gather(k_block, "req", axis=0, tiled=True),
        lax.all_gather(v_block, "req", axis=0, tiled=True),
        lax.all_gather(o_block, "req", axis=0, tiled=True),
    )
    x32 = hidden[0].astype(jnp.float32)
    mean = jnp.mean(x32, axis=-1, keepdims=True)
    centered = x32 - mean
    var = jnp.mean(centered * centered, axis=-1, keepdims=True)
    normed = (centered * lax.rsqrt(var + 1e-06) * norm_gain).astype(jnp.bfloat16)
    kv_local = jnp.concatenate([k_local, v_local], axis=1)
    new_kv = jnp.einsum(
        "crd,de->cre",
        lax.all_gather(text_rows, "tp", axis=1, tiled=True),
        kv_local,
        preferred_element_type=jnp.float32,
    ).astype(jnp.bfloat16)
    query = jnp.dot(normed, q_local, preferred_element_type=jnp.float32).astype(jnp.bfloat16)
    selector = text_index[0][None, :] == jnp.arange(text_total, dtype=jnp.int32)[:, None]
    covered = jnp.any(selector, axis=1)
    placed = jnp.dot(
        selector.astype(jnp.bfloat16), new_kv[0], preferred_element_type=jnp.float32
    ).astype(jnp.bfloat16)
    keys = jnp.where(covered[:, None], placed[:, :head_width], key_cache[0])
    values = jnp.where(covered[:, None], placed[:, head_width:], value_cache[0])
    score = lax.dot_general(
        query, keys, (((1,), (1,)), ((), ())), preferred_element_type=jnp.float32
    ) * (1.0 / math.sqrt(head_width))
    valid = jnp.arange(text_total, dtype=jnp.int32) < text_len[0]
    score = jnp.where(valid[None, :], score, -1e30)
    top = jnp.max(score, axis=-1, keepdims=True)
    expo = jnp.exp(score - top)
    weights = (expo / jnp.sum(expo, axis=-1, keepdims=True)).astype(jnp.bfloat16)
    attended = jnp.dot(weights, values, preferred_element_type=jnp.float32).astype(jnp.bfloat16)
    tp_count = lax.axis_size("tp")
    local_rows = hidden.shape[1] // tp_count
    first_row = lax.axis_index("tp") * local_rows
    summed = lax.psum_scatter(
        lax.dot_general(
            attended, o_local, (((1,), (1,)), ((), ())), preferred_element_type=jnp.float32
        ).astype(jnp.bfloat16),
        "tp",
        scatter_dimension=0,
        tiled=True,
    ).astype(jnp.float32)
    own_rows = lax.dynamic_slice_in_dim(x32, first_row, local_rows, 0)
    positions = first_row + jnp.arange(local_rows, dtype=jnp.int32)
    live = positions < clip_len[0]
    result = own_rows + jnp.where(live[:, None], summed, 0.0)
    return result.astype(jnp.bfloat16)[None]


MESH = pl.DeviceIdType.MESH
BF16 = jnp.bfloat16
F32 = jnp.float32


def flip(index, mask):
    result = 0
    for bit in (1, 2, 4):
        has = (index // bit) % 2
        result = result + bit * ((1 - has) if mask & bit else has)
    return result


def fused_kernel(
    hidden_hbm,
    gain,
    qw,
    kw,
    vw,
    ow,
    kc,
    vc,
    text,
    tidx,
    clen,
    tlen,
    out,
    hidden,
    freshbuf,
    selector,
    covering,
    wsend,
    wall,
    tall,
    oall,
    normed,
    resid,
    att,
    ftot,
    fsend,
    frecv,
    w_ss,
    w_rs,
    x_ss,
    t_ss,
    t_rs,
    o_ss,
    o_rs,
    a_ss,
    a_rs,
    f_ss,
    f_rs,
    h_sem,
):
    slots, width = hidden.shape
    block = qw.shape[0]
    text_total, hd = kc.shape
    r = lax.axis_index("req")
    t = lax.axis_index("tp")
    z, y = t // 2, t % 2
    r1 = r + 1 - 2 * (r % 2)
    r2 = (r + 2) % 4
    r3 = (r1 + 2) % 4
    me = r * 8 + t

    def send(src, dst, ss, rs, **dev):
        return pltpu.make_async_remote_copy(
            src_ref=src, dst_ref=dst, send_sem=ss, recv_sem=rs, device_id=dev, device_id_type=MESH
        )

    barrier = pltpu.get_barrier_semaphore()
    for i in range(1, 8):
        pl.semaphore_signal(barrier, inc=1, device_id={"tp": flip(t, i)}, device_id_type=MESH)
    for peer in (r1, r2):
        pl.semaphore_signal(barrier, inc=1, device_id={"req": peer}, device_id_type=MESH)

    hidden_copy = pltpu.make_async_copy(hidden_hbm, hidden, h_sem)
    hidden_copy.start()
    tall[y, z] = text[...]
    for h in range(8):
        cols = slice(h * hd, (h + 1) * hd)
        wsend[h] = jnp.concatenate(
            [qw[:, cols].astype(BF16), kw[:, cols].astype(BF16), vw[:, cols].astype(BF16)], axis=1
        )
    wall[me] = wsend[t]
    oall[r] = ow[...].astype(BF16)
    pl.semaphore_wait(barrier, 9)

    def chain_copy(ref, ss, rs, part, shard, way, sem):
        target = 2 * z + 1 - y if way == 0 else 2 * (z + way) + y
        piece = ref(y, shard, part)
        slot = rs.shape[0] // 8 * (4 * y + shard) + part
        return send(piece, piece, ss.at[sem], rs.at[slot], tp=target)

    def chain_step(ref, ss, rs, part, d, wait_send=False, then=None):
        parts = rs.shape[0] // 8
        for side in (1, -1):
            if d == 0 and side == -1:
                continue
            shard = z - side * d
            base = 3 * (parts * (2 * d + (side < 0)) + part)

            @pl.when((shard >= 0) & (shard <= 3))
            def _():
                across = chain_copy(ref, ss, rs, part, shard, 0, base)
                if d > 0 and not wait_send:
                    across.wait_recv()
                for way in (1, -1):
                    if d > 0 and way != side:
                        continue
                    onward = chain_copy(
                        ref, ss, rs, part, shard, way, base + (1 if way == 1 else 2)
                    )

                    @pl.when((z + way >= 0) & (z + way <= 3))
                    def _():
                        if wait_send:
                            onward.wait_send()
                        else:
                            onward.start()

                if wait_send:
                    across.wait_send()
                else:
                    across.start()
                if then is not None:
                    then(y, shard)

    def crossed(ref, ss, rs, part, shard):
        piece = ref(1 - y, shard, part)
        slot = rs.shape[0] // 8 * (4 * (1 - y) + shard) + part
        send(piece, piece, ss.at[0], rs.at[slot], tp=flip(t, 1)).wait_recv()

    def text_ref(column, shard, part):
        return tall.at[column, shard, part]

    def att_ref(column, shard, part):
        return att.at[2 * shard + column]

    def text_step(d, wait_send=False):
        for part in range(2):
            chain_step(text_ref, t_ss, t_rs, part, d, wait_send)

    text_step(0)

    o_copies = [
        send(oall.at[r], oall.at[r], o_ss.at[0], o_rs.at[r], req=r1),
        send(oall.at[r], oall.at[r], o_ss.at[1], o_rs.at[r], req=r2),
        send(oall.at[r2], oall.at[r2], o_ss.at[2], o_rs.at[r2], req=r1),
    ]
    w_copies = [
        send(wsend.at[flip(t, i)], wall.at[me], w_ss.at[i], w_rs.at[me], tp=flip(t, i))
        for i in range(1, 8)
    ]

    def onward(i, which):
        if which == 2:
            slot, target = r2 * 8 + flip(t, i), r1
        else:
            slot, target = r * 8 + flip(t, i), (r1 if which == 0 else r2)
        return send(wall.at[slot], wall.at[slot], x_ss.at[8 * which + i], w_rs.at[slot], req=target)

    def w_arrived(owner, i):
        slot = owner * 8 + flip(t, i)
        send(wall.at[slot], wall.at[slot], w_ss.at[0], w_rs.at[slot], req=r1).wait_recv()

    def o_arrived(owner):
        send(oall.at[owner], oall.at[owner], o_ss.at[0], o_rs.at[owner], req=r1).wait_recv()

    for copy in w_copies[:3]:
        copy.start()
    onward(0, 1).start()
    onward(0, 0).start()
    o_copies[1].start()
    o_copies[0].start()

    def norm_rows(c, carry):
        rows = pl.ds(pl.multiple_of(c * 16, 16), 16)
        x = hidden[rows, :].astype(F32)
        mean = jnp.mean(x, axis=-1, keepdims=True)
        centered = x - mean
        var = jnp.mean(centered * centered, axis=-1, keepdims=True)
        normed[rows, :] = (centered * lax.rsqrt(var + 1e-06) * gain[...]).astype(BF16)
        return carry


    text_step(1)
    for copy in w_copies[3:]:
        copy.start()
    for i in (1, 2, 3):
        w_arrived(r, i)
        onward(i, 1).start()
        onward(i, 0).start()
    text_step(2)
    for i in (4, 5, 6, 7):
        w_arrived(r, i)
        onward(i, 1).start()
        onward(i, 0).start()
    text_step(3)

    hidden_copy.wait()
    lax.fori_loop(0, slots // 16, norm_rows, 0)
    span = 8 * block
    picked = (
        lax.broadcasted_iota(jnp.int32, (span, block), 0)
        == lax.broadcasted_iota(jnp.int32, (span, block), 1) + t * block
    )
    pick = jnp.where(picked, 1.0, 0.0).astype(BF16)
    resid[...] = jnp.concatenate(
        [
            jnp.dot(hidden[:, g * span : (g + 1) * span], pick, preferred_element_type=F32)
            for g in range(4)
        ],
        axis=1,
    )
    recomp = tidx.shape[1]
    row = lax.broadcasted_iota(jnp.int32, (text_total, recomp), 0)
    chosen = jnp.where(tidx[...] == row, 1.0, 0.0)
    selector[...] = chosen.astype(BF16)
    covering[...] = jnp.broadcast_to(jnp.sum(chosen, axis=1, keepdims=True), covering.shape)

    def query_part(g):
        return jnp.dot(
            normed[:, pl.ds(pl.multiple_of(g * span, span), span)],
            wall[pl.ds(8 * g, 8), :, 0:hd].reshape(span, hd),
            preferred_element_type=F32,
        )

    for i in range(8):
        w_arrived(r2, i)
        onward(i, 2).start()
    o_arrived(r2)
    o_copies[2].start()
    query = query_part(r) + query_part(r2)
    for i in range(8):
        w_arrived(r1, i)
    query += query_part(r1)
    for i in range(8):
        w_arrived(r3, i)
    query += query_part(r3)
    query = query.astype(BF16)

    shard_rows = text.shape[0] * text.shape[1]

    def fresh_rows(column):
        lines = tall[column].reshape(4 * shard_rows, 4 * span)
        part = jnp.dot(
            lines, wall[:, :, hd : 3 * hd].reshape(4 * span, 2 * hd), preferred_element_type=F32
        ).astype(BF16)
        for shard in range(4):
            freshbuf[2 * shard + column] = part[shard * shard_rows : (shard + 1) * shard_rows]

    fresh_rows(y)
    for shard in range(4):
        for part in range(2):
            crossed(text_ref, t_ss, t_rs, part, shard)
    fresh_rows(1 - y)
    fresh = freshbuf[...].reshape(recomp, 2 * hd)

    covered = covering[...] > 0.5
    placed = jnp.dot(selector[...], fresh, preferred_element_type=F32)
    keys = jnp.where(covered, placed[:, :hd], kc[...].astype(F32)).astype(BF16)
    values = jnp.where(covered, placed[:, hd:], vc[...].astype(F32)).astype(BF16)
    score = lax.dot_general(query, keys, (((1,), (1,)), ((), ())), preferred_element_type=F32)
    score = score * (1.0 / math.sqrt(hd))
    column = lax.broadcasted_iota(jnp.int32, score.shape, 1)
    score = jnp.where(column < tlen[0], score, -1e30)
    top = jnp.max(score, axis=-1, keepdims=True)
    expo = jnp.exp(score - top)
    weights = (expo / jnp.sum(expo, axis=-1, keepdims=True)).astype(BF16)
    att[t] = jnp.dot(weights, values, preferred_element_type=F32).astype(BF16)

    chain_step(att_ref, a_ss, a_rs, 0, 0)
    o_arrived(r1)
    o_arrived(r3)
    local = slots // 8
    step = 2 * local
    features = 4 * block

    def head_rows(slot, c):
        rows = pl.ds(pl.multiple_of(c * step, 16), step)
        head = pl.ds(pl.multiple_of(slot * hd, hd), hd)
        term = lax.dot_general(
            att[slot, rows, :],
            oall[:, :, head].reshape(features, hd),
            (((1,), (1,)), ((), ())),
            preferred_element_type=F32,
        )
        return rows, term.astype(BF16).astype(F32)

    def add_head(column, shard):
        def body(c, carry):
            rows, term = head_rows(2 * shard + column, c)
            ftot[rows, :] += term
            return carry

        lax.fori_loop(0, 4, body, 0)

    ftot[...] = jnp.zeros_like(ftot)
    add_head(y, z)
    for d in (1, 2, 3):
        chain_step(att_ref, a_ss, a_rs, 0, d, then=add_head)

    def z_flip(mask):
        return flip(t, 2 * mask) // 2

    for m in (0, 1, 3, 2):
        crossed(att_ref, a_ss, a_rs, 0, z_flip(m))
        if m != 2:
            add_head(1 - y, z_flip(m))

    tiles = features // 128
    padded = fsend.shape[1]
    f_copies = []
    for m in (3, 2, 1, 0):
        c = z_flip(m)
        rows, term = head_rows(2 * z_flip(2) + 1 - y, c)
        total = ftot[rows, :] + term
        position = lax.broadcasted_iota(jnp.int32, total.shape, 0) + c * step
        total = resid[rows, :] + jnp.where(position < clen[0], total, 0.0)
        for half in range(2):
            own = total[half * local : (half + 1) * local]
            pieces = [own[:, k * 128 : (k + 1) * 128] for k in range(tiles)]
            if padded > tiles * local:
                pieces.append(jnp.zeros((padded - tiles * local, 128), F32))
            fsend[2 * c + half] = jnp.concatenate(pieces, axis=0).astype(BF16)
        for i in (2 * m, 2 * m + 1):
            if i > 0:
                copy = send(
                    fsend.at[flip(t, i)], frecv.at[t], f_ss.at[i], f_rs.at[t], tp=flip(t, i)
                )
                copy.start()
                f_copies.append(copy)
    frecv[t] = fsend[t]
    for i in range(1, 8):
        slot = flip(t, i)
        send(frecv.at[slot], frecv.at[slot], f_ss.at[0], f_rs.at[slot], tp=slot).wait_recv()
    lines = []
    for j in range(8):
        got = frecv[j].astype(F32)
        lines.append(
            jnp.concatenate([got[k * local : (k + 1) * local] for k in range(tiles)], axis=1)
        )
    for g in range(4):
        pieces = [line[:, g * block : (g + 1) * block] for line in lines]
        out[:, g * span : (g + 1) * span] = jnp.concatenate(pieces, axis=1).astype(BF16)

    for d in range(4):
        text_step(d, wait_send=True)
        chain_step(att_ref, a_ss, a_rs, 0, d, wait_send=True)
    for copy in w_copies + o_copies + f_copies:
        copy.wait_send()
    for which in range(3):
        for i in range(8):
            onward(i, which).wait_send()


def fused(hidden, gain, qw, kw, vw, ow, kc, vc, text, tidx, clen, tlen):
    _, slots, width = hidden.shape
    block, inner = qw.shape
    _, text_total, hd = kc.shape
    local = slots // 8
    tiles = 4 * block // 128
    padded = -(-tiles * local // 16) * 16
    pieces = text[0].reshape(2, text.shape[1] // 2, width)
    vmem = pl.BlockSpec(memory_space=pltpu.VMEM)
    smem = pl.BlockSpec(memory_space=pltpu.SMEM)
    dma = pltpu.SemaphoreType.DMA
    result = pl.pallas_call(
        fused_kernel,
        out_shape=jax.ShapeDtypeStruct((local, width), BF16),
        in_specs=[pl.BlockSpec(memory_space=pltpu.HBM)] + [vmem] * 9 + [smem] * 2,
        out_specs=vmem,
        scratch_shapes=[
            pltpu.VMEM((slots, width), BF16),
            pltpu.VMEM((8, text.shape[1], 2 * hd), BF16),
            pltpu.VMEM((text_total, tidx.shape[1]), BF16),
            pltpu.VMEM((text_total, hd), F32),
            pltpu.VMEM((8, block, 3 * hd), BF16),
            pltpu.VMEM((32, block, 3 * hd), BF16),
            pltpu.VMEM((2, 4, *pieces.shape), BF16),
            pltpu.VMEM((4, block, inner), BF16),
            pltpu.VMEM((slots, width), BF16),
            pltpu.VMEM((slots, 4 * block), F32),
            pltpu.VMEM((8, slots, hd), BF16),
            pltpu.VMEM((slots, 4 * block), F32),
            pltpu.VMEM((8, padded, 128), BF16),
            pltpu.VMEM((8, padded, 128), BF16),
            dma((8,)),
            dma((32,)),
            dma((24,)),
            dma((48,)),
            dma((16,)),
            dma((3,)),
            dma((4,)),
            dma((24,)),
            dma((8,)),
            dma((8,)),
            dma((8,)),
            dma(()),
        ],
        compiler_params=pltpu.CompilerParams(
            collective_id=0, has_side_effects=True, vmem_limit_bytes=56 * 1024 * 1024
        ),
        cost_estimate=pl.CostEstimate(
            flops=3 * 10**9, bytes_accessed=10**7, transcendentals=slots * text_total
        ),
    )(
        hidden[0], gain[None], qw, kw, vw, ow, kc[0], vc[0], pieces, tidx, clen, tlen
    )
    return result[None]


def solution(mesh):
    def run(*args):
        hidden, qw, text = args[0], args[2], args[8]
        fits = (
            (mesh.shape["req"], mesh.shape["tp"]) == (4, 8)
            and qw.shape[0] % 16 == 0
            and text.shape[1] % 32 == 0
            and qw.shape[0] % 32 == 0
            and hidden.shape[1] % 80 == 0
        )
        return (fused if fits else on_device)(*args)

    return jax.shard_map(
        run,
        mesh=mesh,
        in_specs=(
            P("req", None, None),
            P(),
            P(("req", "tp"), None),
            P(("req", "tp"), None),
            P(("req", "tp"), None),
            P(("req", "tp"), None),
            P("req", None, "tp"),
            P("req", None, "tp"),
            P("req", "tp", None),
            P("req", None),
            P("req"),
            P("req"),
        ),
        out_specs=P("req", "tp", None),
        check_vma=False,
    )
```
